32 devices in a mesh: ifg: 16 (over z, y, x), tile: 2 (over core).
Axes of the slice: x: 2, y: 2, z: 4, core: 2. Of those that a mesh axis runs over, the one named last changes fastest.
Arguments:
- phases: float32 [1024, 128, 64], P('ifg', 'tile'), may hold values from -6 to 6
- pairs: int32 [1024, 2], replicated, may hold values from 0 to 299, as said below
- class_weights: float32 [8, 1024], replicated, may hold values from 0.05 to 1
- classes: int32 [128, 64], P('tile', 'ifg'), may hold values from 0 to 7
Outputs:
- corrected: float32 [128, 64, 300], P('tile', 'ifg')
The draws below stay inside these ranges and needn't reach their ends.
Inputs may be any that keep to these rules, and one draw needn't show every extreme that they name: pairs[i,0] < pairs[i,1] <= pairs[i,0] + 8; some interferogram starts at date 0 and some ends at date 300 - 1.
All inputs are finite; a program needn't handle non-finite values.
Results may differ from the reference program's by a relative error of at most 0.0003.
Values sent between devices are 32-bit elements; how exact they have to be, the bound alone decides.
A program may use at most 128 MiB of HBM per device.

```python
import math
import jax
import jax.numpy as jnp
from jax import lax

DATES = 300
NIFG = 1024
CLASSES = 8
MAXGAP = 8
R = 3
ROWS = 128
COLS = 64


def draw_pairs(key, part):
    first_key, second_key = jax.random.split(jax.random.fold_in(key, 17))
    first = jax.random.randint(first_key, (NIFG,), 0, DATES - 1)
    first = first.at[0].set(0).at[NIFG - 1].set(DATES - 2)
    spacing = jax.random.randint(second_key, (NIFG,), 1, MAXGAP + 1)
    second = jnp.minimum(first + spacing, DATES - 1)
    return jnp.stack([first, second], axis=1).astype(jnp.int32)


def plant(values, own_key, least, high):
    extent = values.shape
    index_at = [jax.random.randint(jax.random.fold_in(own_key, axis), (), 0, extent[axis]) for axis in range(len(extent))]
    values = values.at[tuple(index_at)].set(least)
    longest = extent.index(max(extent))
    index_at[longest] = (index_at[longest] + 1) % extent[longest]
    return values.at[tuple(index_at)].set(high)


def steps_of(stream_key, extent, pieces, least, high):
    gain, own = 1.0, jax.random.fold_in(stream_key, 6)
    for axis_at, parts in pieces:
        steps = jnp.exp(jax.random.uniform(jax.random.fold_in(own, axis_at), (parts,), jnp.float32, least / len(pieces), high / len(pieces)))
        gain = gain * jnp.repeat(steps, extent[axis_at] // parts).reshape([-1 if axis == axis_at else 1 for axis in range(len(extent))])
    return gain


def noise(own_key, shape, deviation, reach, cuts=(), held_as=jnp.bfloat16):
    entries = jax.random.normal(own_key, shape, jnp.float32) * deviation
    if len(cuts) > 0:
        entries = steps_of(own_key, shape, cuts, -0.22, 0.18) * entries
    return jnp.clip(entries, min=-reach, max=reach).astype(held_as)


def setup_inputs(seed: int = 0) -> dict:
    key_of = jax.random.split(jax.random.key(seed), 5)
    phases = noise(key_of[0], (NIFG, ROWS, COLS), 1.0, 6.0, ((0, 16), (1, 2)), jnp.float32)
    pairs = draw_pairs(jax.random.fold_in(key_of[4], 71), 0)
    class_weights = jnp.clip(jnp.exp(jax.random.uniform(key_of[2], (CLASSES, NIFG), jnp.float32, math.log(0.05), math.log(1.0))), 0.05, 1.0)
    classes = plant(jax.random.randint(key_of[3], (ROWS, COLS), 0, CLASSES), jax.random.fold_in(key_of[3], 1), 0, CLASSES - 1).astype(jnp.int32)
    return dict(phases=phases, pairs=pairs, class_weights=class_weights, classes=classes)


smooth_weight = 1.0
anchor_weight = 0.1

def incidence_matrix(pairs):
    dates = jnp.arange(DATES, dtype=jnp.int32)[:, None]
    plus = (dates == pairs[:, 1][None, :]).astype(jnp.float32)
    minus = (dates == pairs[:, 0][None, :]).astype(jnp.float32)
    return plus - minus

def prior_matrix():
    second = jnp.arange(DATES - 2, dtype=jnp.int32)[:, None]
    columns = jnp.arange(DATES, dtype=jnp.int32)[None, :]
    diffs = (columns == second).astype(jnp.float32) - 2.0 * (columns == second + 1).astype(jnp.float32) + (columns == second + 2).astype(jnp.float32)
    curvature = jnp.dot(diffs.T.astype(jnp.float32), diffs.astype(jnp.float32), precision=lax.Precision.HIGHEST, preferred_element_type=jnp.float32)
    return smooth_weight * curvature + anchor_weight * jnp.eye(DATES, dtype=jnp.float32)

def invert(matrix):
    factor = jnp.linalg.cholesky(matrix)
    return jax.scipy.linalg.cho_solve((factor, True), jnp.eye(DATES, dtype=jnp.float32))

def filter_taps():
    offsets = jnp.arange(-R, R + 1).astype(jnp.float32)
    values = jnp.exp(-offsets * offsets / 4.5)
    return values / jnp.sum(values)

def reference(phases, pairs, class_weights, classes):
    incidence = incidence_matrix(pairs)
    normal = jnp.einsum('di,ki,ei->kde', incidence, class_weights, incidence, precision=lax.Precision.HIGHEST)
    inverse = jax.vmap(invert)(normal + prior_matrix()[None])

    def invert_row(row_index):
        phase_row = lax.dynamic_slice_in_dim(phases, row_index, 1, 1)[:, 0, :]
        class_row = lax.dynamic_slice_in_dim(classes, row_index, 1, 0)[0]
        onehot = (class_row[None, :] == jnp.arange(CLASSES, dtype=jnp.int32)[:, None]).astype(jnp.float32)
        pixel_weights = jnp.dot(class_weights.T.astype(jnp.float32), onehot.astype(jnp.float32), precision=lax.Precision.HIGHEST, preferred_element_type=jnp.float32)
        right_terms = jnp.einsum('ip,di->pd', pixel_weights * phase_row, incidence, precision=lax.Precision.HIGHEST)
        result = jnp.zeros((COLS, DATES), jnp.float32)
        for member in range(CLASSES):
            solved = jnp.einsum('pd,ed->pe', right_terms, inverse[member], precision=lax.Precision.HIGHEST)
            result = result + onehot[member][:, None] * solved
        return result
    displacement = lax.map(invert_row, jnp.arange(ROWS, dtype=jnp.int32))
    filter_weights = filter_taps()
    padded = jnp.pad(displacement, ((R, R), (R, R), (0, 0)))
    across = filter_weights[0] * padded[:, 0:COLS]
    for offset in range(1, 2 * R + 1):
        across = across + filter_weights[offset] * padded[:, offset:offset + COLS]
    atmosphere = filter_weights[0] * across[0:ROWS]
    for offset in range(1, 2 * R + 1):
        atmosphere = atmosphere + filter_weights[offset] * across[offset:offset + ROWS]
    return displacement - atmosphere
```

```python
import functools
import jax
import jax.numpy as jnp
from jax import lax
from jax.experimental import pallas as pl
from jax.experimental.pallas import tpu as pltpu
from jax.sharding import PartitionSpec as P

DATES = 300
CLASSES = 8
MAXGAP = 8
R = 3
LANES = 128
PAD = -(-DATES // 8) * 8
MESH = pl.DeviceIdType.MESH
HIGHEST = lax.Precision.HIGHEST

smooth_weight = 1.0
anchor_weight = 0.1


def split3(value):
    high = value.astype(jnp.bfloat16)
    rest = value - high.astype(jnp.float32)
    middle = rest.astype(jnp.bfloat16)
    low = (rest - middle.astype(jnp.float32)).astype(jnp.bfloat16)
    return (high, middle, low)


def dot_nt(a, b, **kw):
    return lax.dot_general(a, b, (((1,), (1,)), ((), ())), preferred_element_type=jnp.float32, **kw)


def dot_nn(a, b, **kw):
    return lax.dot_general(a, b, (((1,), (0,)), ((), ())), preferred_element_type=jnp.float32, **kw)


def factor_kernel(pairs_ref, w_ref, wt_ref, cls_ref, inc_ref, wpx_ref, lpx_ref, band, low):
    nifg = pairs_ref.shape[1]
    pixels = cls_ref.shape[1]
    first = pairs_ref[0:1, :]
    second = pairs_ref[1:2, :]
    gap = second - first
    dates = lax.broadcasted_iota(jnp.int32, (PAD, nifg), 0)
    minus_f = jnp.where(dates == first, 1.0, 0.0)
    plus_f = jnp.where(dates == second, 1.0, 0.0)
    inc_ref[...] = (plus_f - minus_f).astype(jnp.bfloat16)
    minus = minus_f.astype(jnp.bfloat16)
    both = (plus_f + minus_f).astype(jnp.bfloat16)
    w = w_ref[...]
    row = lax.broadcasted_iota(jnp.int32, (PAD, LANES), 0)
    inside = lambda ok: jnp.where(ok, 1.0, 0.0)
    for g in range(MAXGAP + 1):
        parts = split3(w if g == 0 else jnp.where(gap == g, w, 0.0))
        left = both if g == 0 else minus
        total = dot_nt(left, parts[0]) + (dot_nt(left, parts[1]) + dot_nt(left, parts[2]))
        here = inside(row <= DATES - 3)
        before = inside((row >= 1) & (row <= DATES - 2))
        if g == 0:
            twice = inside((row >= 2) & (row <= DATES - 1))
            prior = smooth_weight * (here + 4.0 * before + twice) + anchor_weight
            total = total + jnp.where(row < DATES, prior, 1.0)
        elif g == 1:
            total = smooth_weight * (-2.0 * here - 2.0 * before) - total
        elif g == 2:
            total = smooth_weight * here - total
        else:
            total = -total
        band[g] = total

    zero = jnp.zeros((1, LANES), jnp.float32)
    keys = [(j, h) for j in range(MAXGAP) for h in range(MAXGAP - j)]

    def factor_block(block, carry):
        acc = dict(zip(keys, carry))
        base = pl.multiple_of(block * 8, 8)
        for s in range(8):
            at = pl.ds(base + s, 1)
            c = [band[h, at, :] for h in range(MAXGAP + 1)]
            c = [c[h] - acc[(0, h)] for h in range(MAXGAP)] + [c[MAXGAP]]
            inv = 1.0 / c[0]
            low[0, at, :] = inv
            fresh = {}
            for j in range(1, MAXGAP + 1):
                lj = c[j] * inv
                low[j, at, :] = lj
                for h in range(MAXGAP - j + 1):
                    term = lj * c[j + h]
                    old = acc.get((j, h))
                    fresh[(j - 1, h)] = term if old is None else old + term
            acc = fresh
        return tuple(acc[k] for k in keys)

    lax.fori_loop(0, PAD // 8, factor_block, tuple(zero for _ in keys))

    member = lax.broadcasted_iota(jnp.int32, (LANES, pixels), 0)
    onehot = jnp.where(member == cls_ref[...], 1.0, 0.0).astype(jnp.bfloat16)

    def expand(value):
        parts = split3(value)
        return dot_nn(parts[0], onehot) + (dot_nn(parts[1], onehot) + dot_nn(parts[2], onehot))

    for g in range(MAXGAP + 1):
        lpx_ref[g] = expand(low[g])
    wpx_ref[...] = expand(wt_ref[...])


def solve_kernel(recv_ref, inc_ref, wpx_ref, lpx_ref, self_ref, left_ref, right_ref, sel_ref,
                 tile_ref, out_ref, rows, x_ref, edge, halo_left, halo_right, halo_tile,
                 send_sem, recv_sem):
    me = lax.axis_index("ifg")
    core = lax.axis_index("tile")
    count = lax.axis_size("ifg")
    left = lax.rem(me + count - 1, count)
    right = lax.rem(me + 1, count)
    other = 1 - core
    partners = [(left, core), (right, core), (me, other), (left, other), (right, other)]
    barrier = pltpu.get_barrier_semaphore()
    for partner in partners:
        pl.semaphore_signal(barrier, inc=1, device_id=partner, device_id_type=MESH)
    pl.semaphore_wait(barrier, len(partners))

    parts = split3(recv_ref[...] * wpx_ref[...])
    inc = inc_ref[...]
    pixels = x_ref.shape[1]
    rows[0:PAD, :] = dot_nn(inc, parts[0]) + (dot_nn(inc, parts[1]) + dot_nn(inc, parts[2]))
    rows[PAD:PAD + 8, :] = jnp.zeros((8, pixels), jnp.float32)

    def forward(block, carry):
        a = list(carry)
        base = pl.multiple_of(block * 8, 8)
        for s in range(8):
            at = pl.ds(base + s, 1)
            y = a[0]
            a = a[1:] + [rows[pl.ds(base + s + 8, 1), :]]
            a = [a[j] - lpx_ref[j + 1, at, :] * y for j in range(8)]
            x_ref[at, :] = y * lpx_ref[0, at, :]
        return tuple(a)

    lax.fori_loop(0, PAD // 8, forward, tuple(rows[d:d + 1, :] for d in range(8)))

    def backward(block, carry):
        later = list(carry)
        base = pl.multiple_of(PAD - 8 - block * 8, 8)
        for s in range(7, -1, -1):
            at = pl.ds(base + s, 1)
            value = x_ref[at, :]
            for g in range(8, 0, -1):
                value = value - lpx_ref[g, at, :] * later[g - 1]
            x_ref[at, :] = value
            later = [value] + later[:7]
        return tuple(later)

    lax.fori_loop(0, PAD // 8, backward, tuple(jnp.zeros((1, pixels), jnp.float32) for _ in range(8)))

    def copy(i, src, dst, device):
        return pltpu.make_async_remote_copy(src_ref=src, dst_ref=dst, send_sem=send_sem.at[i],
                                            recv_sem=recv_sem.at[i], device_id=device,
                                            device_id_type=MESH)

    copies = [copy(0, x_ref, halo_right, (left, core)), copy(1, x_ref, halo_left, (right, core))]
    for c in copies:
        c.start()
    x = x_ref[...]
    edge[...] = dot_nt(sel_ref[...], x, precision=HIGHEST)
    small = [copy(2, edge, halo_tile.at[1], (me, other)),
             copy(3, edge, halo_tile.at[2], (left, other)),
             copy(4, edge, halo_tile.at[0], (right, other))]
    for c in small:
        c.start()
    total = dot_nt(self_ref[...], x, precision=HIGHEST)
    for c in small:
        c.wait()
    for i in range(3):
        total += dot_nn(tile_ref[i], halo_tile[i], precision=HIGHEST)
    copies[0].wait()
    total += dot_nt(right_ref[...], halo_right[...], precision=HIGHEST)
    copies[1].wait()
    total += dot_nt(left_ref[...], halo_left[...], precision=HIGHEST)
    out_ref[...] = total[:, 0:DATES]


def filter_taps():
    offsets = jnp.arange(-R, R + 1).astype(jnp.float32)
    return jnp.sum(jnp.exp(-offsets * offsets / 4.5))


def tap(delta, norm):
    near = jnp.exp(-(delta * delta).astype(jnp.float32) / 4.5) / norm
    return jnp.where(jnp.abs(delta) <= R, near, 0.0)


def filter_matrices(tile_rows, tile_cols):
    norm = filter_taps()
    pixels = tile_rows * tile_cols
    me, core = lax.axis_index("ifg"), lax.axis_index("tile")
    count = lax.axis_size("ifg")
    out = jnp.arange(pixels, dtype=jnp.int32)[:, None]
    out_r, out_c = out // tile_cols, out % tile_cols
    inn = jnp.arange(pixels, dtype=jnp.int32)[None, :]
    in_c, in_r = inn // tile_rows, inn % tile_rows
    vertical = tap(out_r - in_r, norm)
    has_left = jnp.where(me > 0, 1.0, 0.0)
    has_right = jnp.where(me < count - 1, 1.0, 0.0)
    same = jnp.where((out_r == in_r) & (out_c == in_c), 1.0, 0.0)
    own = same - vertical * tap(out_c - in_c, norm)
    left = -has_left * vertical * tap(out_c - in_c + tile_cols, norm)
    right = -has_right * vertical * tap(out_c - in_c - tile_cols, norm)
    slot = jnp.arange(16, dtype=jnp.int32)
    slot_c, slot_j = slot // 4, slot % 4
    sent_r = jnp.where(core == 0, tile_rows - R + slot_j, slot_j)
    sel = jnp.where((slot_j[:, None] < R) & (sent_r[:, None] == in_r) & (slot_c[:, None] == in_c), 1.0, 0.0)
    got_r = jnp.where(core == 0, tile_rows + slot_j, slot_j - R)[None, :]
    reach = jnp.where(slot_j[None, :] < R, tap(out_r - got_r, norm), 0.0)
    tiles = jnp.stack([
        -has * reach * tap(out_c - slot_c[None, :] + shift, norm)
        for has, shift in ((has_left, tile_cols), (1.0, 0), (has_right, -tile_cols))
    ])
    return own, left, right, sel, tiles


def on_device(phases, pairs, class_weights, classes):
    own_ifg, tile_rows, cols = phases.shape
    tile_cols = classes.shape[1]
    pixels = tile_rows * tile_cols
    count = cols // tile_cols
    nifg = pairs.shape[0]
    vmem = pl.BlockSpec(memory_space=pltpu.VMEM)

    blocks = phases.transpose(0, 2, 1).reshape(own_ifg, count, pixels).transpose(1, 0, 2)
    received = lax.all_to_all(blocks, "ifg", split_axis=0, concat_axis=0, tiled=True)
    received = received.reshape(nifg, pixels)

    padded = jnp.pad(class_weights, ((0, LANES - CLASSES), (0, 0)))
    inc, wpx, lpx = pl.pallas_call(
        factor_kernel,
        out_shape=(
            jax.ShapeDtypeStruct((PAD, nifg), jnp.bfloat16),
            jax.ShapeDtypeStruct((nifg, pixels), jnp.float32),
            jax.ShapeDtypeStruct((MAXGAP + 1, PAD, pixels), jnp.float32),
        ),
        in_specs=[vmem] * 4,
        out_specs=(vmem,) * 3,
        scratch_shapes=[
            pltpu.VMEM((MAXGAP + 1, PAD, LANES), jnp.float32),
            pltpu.VMEM((MAXGAP + 1, PAD, LANES), jnp.float32),
        ],
        compiler_params=pltpu.CompilerParams(vmem_limit_bytes=40 * 1024 * 1024),
        cost_estimate=pl.CostEstimate(flops=40_000_000_000, bytes_accessed=6_000_000, transcendentals=0),
        name="factor",
    )(pairs.T, padded, padded.T, classes.T.reshape(1, pixels))

    own, left, right, sel, tiles = filter_matrices(tile_rows, tile_cols)
    corrected = pl.pallas_call(
        solve_kernel,
        out_shape=jax.ShapeDtypeStruct((pixels, DATES), jnp.float32),
        in_specs=[vmem] * 9,
        out_specs=vmem,
        scratch_shapes=[
            pltpu.VMEM((PAD + 8, pixels), jnp.float32),
            pltpu.VMEM((PAD, pixels), jnp.float32),
            pltpu.VMEM((16, PAD), jnp.float32),
            pltpu.VMEM((PAD, pixels), jnp.float32),
            pltpu.VMEM((PAD, pixels), jnp.float32),
            pltpu.VMEM((3, 16, PAD), jnp.float32),
            pltpu.SemaphoreType.DMA((5,)),
            pltpu.SemaphoreType.DMA((5,)),
        ],
        compiler_params=pltpu.CompilerParams(
            collective_id=0, has_side_effects=True, vmem_limit_bytes=40 * 1024 * 1024
        ),
        name="solve",
    )(received, inc, wpx, lpx, own, left, right, sel, tiles)
    return corrected.reshape(tile_rows, tile_cols, DATES)


def solution(mesh):
    return jax.shard_map(
        on_device,
        mesh=mesh,
        in_specs=(P("ifg", "tile", None), P(), P(), P("tile", "ifg")),
        out_specs=P("tile", "ifg", None),
        check_vma=False,
    )
```

```python
import functools
import math
import jax
import jax.numpy as jnp
from jax import lax
from jax.experimental import pallas as pl
from jax.experimental.pallas import tpu as pltpu
from jax.sharding import PartitionSpec as P

DATES = 300
CLASSES = 8
MAXGAP = 8
R = 3
LANES = 128
PAD = -(-DATES // 8) * 8
CHUNKS = 4
MESH = pl.DeviceIdType.MESH
HIGHEST = lax.Precision.HIGHEST

smooth_weight = 1.0
anchor_weight = 0.1


def split3(value):
    high = value.astype(jnp.bfloat16)
    rest = value - high.astype(jnp.float32)
    middle = rest.astype(jnp.bfloat16)
    low = (rest - middle.astype(jnp.float32)).astype(jnp.bfloat16)
    return (high, middle, low)


def dot_nt(a, b, **kw):
    return lax.dot_general(a, b, (((1,), (1,)), ((), ())), preferred_element_type=jnp.float32, **kw)


def dot_nn(a, b, **kw):
    return lax.dot_general(a, b, (((1,), (0,)), ((), ())), preferred_element_type=jnp.float32, **kw)


def factor(pairs_ref, w_ref, wt_ref, cls_ref, inc_ref, wpx_ref, lpx_ref, band, low):
    nifg = pairs_ref.shape[1]
    pixels = cls_ref.shape[1]
    first = pairs_ref[0:1, :]
    second = pairs_ref[1:2, :]
    gap = second - first
    dates = lax.broadcasted_iota(jnp.int32, (PAD, nifg), 0)
    minus_f = jnp.where(dates == first, 1.0, 0.0)
    plus_f = jnp.where(dates == second, 1.0, 0.0)
    inc_ref[...] = (plus_f - minus_f).astype(jnp.bfloat16)
    minus = minus_f.astype(jnp.bfloat16)
    both = (plus_f + minus_f).astype(jnp.bfloat16)
    w = w_ref[...]
    row = lax.broadcasted_iota(jnp.int32, (PAD, LANES), 0)
    inside = lambda ok: jnp.where(ok, 1.0, 0.0)
    for g in range(MAXGAP + 1):
        parts = split3(w if g == 0 else jnp.where(gap == g, w, 0.0))
        left = both if g == 0 else minus
        total = dot_nt(left, parts[0]) + (dot_nt(left, parts[1]) + dot_nt(left, parts[2]))
        here = inside(row <= DATES - 3)
        before = inside((row >= 1) & (row <= DATES - 2))
        if g == 0:
            twice = inside((row >= 2) & (row <= DATES - 1))
            prior = smooth_weight * (here + 4.0 * before + twice) + anchor_weight
            total = total + jnp.where(row < DATES, prior, 1.0)
        elif g == 1:
            total = smooth_weight * (-2.0 * here - 2.0 * before) - total
        elif g == 2:
            total = smooth_weight * here - total
        else:
            total = -total
        band[g] = total

    zero = jnp.zeros((1, LANES), jnp.float32)
    keys = [(j, h) for j in range(MAXGAP) for h in range(MAXGAP - j)]

    def factor_block(block, carry):
        acc = dict(zip(keys, carry))
        base = pl.multiple_of(block * 8, 8)
        for s in range(8):
            at = pl.ds(base + s, 1)
            c = [band[h, at, :] for h in range(MAXGAP + 1)]
            c = [c[h] - acc[(0, h)] for h in range(MAXGAP)] + [c[MAXGAP]]
            inv = 1.0 / c[0]
            low[0, at, :] = inv
            fresh = {}
            for j in range(1, MAXGAP + 1):
                lj = c[j] * inv
                low[j, at, :] = lj
                for h in range(MAXGAP - j + 1):
                    term = lj * c[j + h]
                    old = acc.get((j, h))
                    fresh[(j - 1, h)] = term if old is None else old + term
            acc = fresh
        return tuple(acc[k] for k in keys)

    lax.fori_loop(0, PAD // 8, factor_block, tuple(zero for _ in keys))

    member = lax.broadcasted_iota(jnp.int32, (LANES, pixels), 0)
    onehot = jnp.where(member == cls_ref[...], 1.0, 0.0).astype(jnp.bfloat16)

    def expand(value):
        parts = split3(value)
        return dot_nn(parts[0], onehot) + (dot_nn(parts[1], onehot) + dot_nn(parts[2], onehot))

    for g in range(MAXGAP + 1):
        lpx_ref[g] = expand(low[g])
    wpx_ref[...] = expand(wt_ref[...])


NORM = sum(math.exp(-j * j / 4.5) for j in range(-R, R + 1))


def tap(delta):
    near = jnp.exp((delta * delta).astype(jnp.float32) * (-1.0 / 4.5)) * (1.0 / NORM)
    return jnp.where(jnp.abs(delta) <= R, near, 0.0)


def split_index(index, size):
    if size & (size - 1):
        return index // size, index % size
    return index >> (size.bit_length() - 1), index & (size - 1)


def iota(shape, dim):
    return lax.broadcasted_iota(jnp.int32, shape, dim)


def fill_filters(tile_rows, tile_cols, own_ref, left_ref, right_ref, sel_ref, tile_ref):
    pixels = tile_rows * tile_cols
    me, core = lax.axis_index("ifg"), lax.axis_index("tile")
    count = lax.axis_size("ifg")
    has_left = jnp.where(me > 0, 1.0, 0.0)
    has_right = jnp.where(me < count - 1, 1.0, 0.0)
    square = (pixels, pixels)
    out_r, out_c = split_index(iota(square, 0), tile_cols)
    in_c, in_r = split_index(iota(square, 1), tile_rows)
    vertical = tap(out_r - in_r)
    same = jnp.where((out_r == in_r) & (out_c == in_c), 1.0, 0.0)
    own_ref[...] = same - vertical * tap(out_c - in_c)
    from_left = jnp.where(in_c >= 2, 1, in_c + 2)
    from_right = jnp.where(in_c >= 2, 2, in_c)
    left = -has_left * vertical * tap(out_c - from_left + tile_cols)
    right = -has_right * vertical * tap(out_c - from_right - tile_cols)
    for ref, value in ((left_ref, left), (right_ref, right)):
        parts = split3(value)
        ref[0] = parts[0]
        ref[1] = parts[1]
    slot_c, slot_j = split_index(iota((16, pixels), 0), 4)
    sel_c, sel_r = split_index(iota((16, pixels), 1), tile_rows)
    sent_r = jnp.where(core == 0, tile_rows - R, 0) + slot_j
    sel_ref[...] = jnp.where((slot_j < R) & (sent_r == sel_r) & (slot_c == sel_c), 1.0, 0.0)
    slot_c, slot_j = split_index(iota((pixels, 16), 1), 4)
    out_r, out_c = split_index(iota((pixels, 16), 0), tile_cols)
    got_r = jnp.where(core == 0, tile_rows, -R) + slot_j
    reach = jnp.where(slot_j < R, tap(out_r - got_r), 0.0)
    tile_ref[0] = -has_left * reach * tap(out_c - slot_c + tile_cols)
    tile_ref[1] = -reach * tap(out_c - slot_c)
    tile_ref[2] = -has_right * reach * tap(out_c - slot_c - tile_cols)


def kernel(tile_rows, tile_cols, blocks_ref, pairs_ref, w_ref, wt_ref, cls_ref, out_ref,
           recv, inc_ref, wpx_ref, lpx_ref, band, low, own_ref, left_ref, right_ref, sel_ref,
           tile_ref, rows, x_ref, spare, edge, halo_pair, halo_spare, halo_tile,
           all_send, all_recv, own_sem, send_sem, recv_sem):
    me = lax.axis_index("ifg")
    core = lax.axis_index("tile")
    count = lax.axis_size("ifg")
    left = lax.rem(me + count - 1, count)
    right = lax.rem(me + 1, count)
    other = 1 - core
    near = [(me, other), (left, other), (right, other)]
    barrier = pltpu.get_barrier_semaphore()

    def greet(k, _):
        pl.semaphore_signal(barrier, inc=1, device_id=(lax.rem(me + k, count), core), device_id_type=MESH)
        return _

    lax.fori_loop(1, count, greet, 0)
    for partner in near:
        pl.semaphore_signal(barrier, inc=1, device_id=partner, device_id_type=MESH)
    pl.semaphore_wait(barrier, count - 1 + len(near))

    def exchange(k, slot):
        peer = lax.rem(me + k, count)
        return pltpu.make_async_remote_copy(
            src_ref=blocks_ref.at[peer], dst_ref=recv.at[slot], send_sem=all_send.at[k],
            recv_sem=all_recv.at[k], device_id=(peer, core), device_id_type=MESH)

    def send_block(k, _):
        exchange(k, me).start()
        return _

    lax.fori_loop(1, count, send_block, 0)
    mine = pltpu.make_async_copy(blocks_ref.at[me], recv.at[me], own_sem)
    mine.start()

    factor(pairs_ref, w_ref, wt_ref, cls_ref, inc_ref, wpx_ref, lpx_ref, band, low)
    fill_filters(tile_rows, tile_cols, own_ref, left_ref, right_ref, sel_ref, tile_ref)

    def take_block(k, _):
        exchange(k, lax.rem(me + count - k, count)).wait()
        return _

    mine.wait()
    lax.fori_loop(1, count, take_block, 0)

    pixels = x_ref.shape[1]
    parts = split3(recv[...].reshape(-1, pixels) * wpx_ref[...])
    inc = inc_ref[...]
    rows[0:PAD, :] = dot_nn(inc, parts[0]) + dot_nn(inc, parts[1])
    rows[PAD:PAD + 8, :] = jnp.zeros((8, pixels), jnp.float32)

    def forward(block, carry):
        a = list(carry)
        base = pl.multiple_of(block * 8, 8)
        for s in range(8):
            at = pl.ds(base + s, 1)
            y = a[0]
            a = a[1:] + [rows[pl.ds(base + s + 8, 1), :]]
            a = [a[j] - lpx_ref[j + 1, at, :] * y for j in range(8)]
            x_ref[at, :] = y * lpx_ref[0, at, :]
        return tuple(a)

    lax.fori_loop(0, PAD // 8, forward, tuple(rows[d:d + 1, :] for d in range(8)))

    def backward(block, carry):
        later = list(carry)
        base = pl.multiple_of(block * 8, 8)
        for s in range(7, -1, -1):
            at = pl.ds(base + s, 1)
            value = x_ref[at, :]
            for g in range(8, 0, -1):
                value = value - lpx_ref[g, at, :] * later[g - 1]
            x_ref[at, :] = value
            later = [value] + later[:7]
        return tuple(later)

    def copy(i, src, dst, device):
        return pltpu.make_async_remote_copy(src_ref=src, dst_ref=dst, send_sem=send_sem.at[i],
                                            recv_sem=recv_sem.at[i], device_id=device,
                                            device_id_type=MESH)

    half = pixels // 2
    total_blocks = PAD // 8
    cuts = [total_blocks * (CHUNKS - i) // CHUNKS for i in range(CHUNKS + 1)]
    carry = tuple(jnp.zeros((1, pixels), jnp.float32) for _ in range(8))
    to_left, to_right = [], []
    for i in range(CHUNKS):
        top, bottom = cuts[i], cuts[i + 1]
        carry = lax.fori_loop(0, top - bottom, lambda n, c, top=top: backward(top - 1 - n, c), carry)
        span = pl.ds(bottom * 8, (top - bottom) * 8)
        to_left.append(copy(2 * i, x_ref.at[span, pl.ds(0, half)], halo_pair.at[1, span], (left, core)))
        to_right.append(copy(2 * i + 1, x_ref.at[span, pl.ds(half, half)], halo_pair.at[0, span], (right, core)))
        to_left[-1].start()
        to_right[-1].start()
    x = x_ref[...]
    mid = PAD // 2
    low_lanes = iota((mid, half), 1) < half // 2
    first, second = x[:, 0:half], x[:, half:]
    spare[0] = jnp.where(low_lanes, pltpu.roll(first[0:mid], half // 2, 1), first[mid:])
    spare[1] = jnp.where(low_lanes, second[0:mid], pltpu.roll(second[mid:], half // 2, 1))
    to_right.append(copy(2 * CHUNKS, spare.at[0], halo_spare.at[0], (right, core)))
    to_left.append(copy(2 * CHUNKS + 1, spare.at[1], halo_spare.at[1], (left, core)))
    to_right[-1].start()
    to_left[-1].start()
    edge[...] = dot_nt(sel_ref[...], x, precision=HIGHEST)
    small = [copy(2 * CHUNKS + 2 + i, edge, halo_tile.at[slot], near[i]) for i, slot in enumerate((1, 2, 0))]
    for c in small:
        c.start()
    total = dot_nt(own_ref[...], x, precision=HIGHEST)
    for c in small:
        c.wait()
    for i in range(3):
        total += dot_nn(tile_ref[i], halo_tile[i], precision=HIGHEST)
    for c in to_right + to_left:
        c.wait()
    keep = (iota((PAD, half), 0) < mid) == (iota((PAD, half), 1) < half // 2)
    for side, ref in ((0, left_ref), (1, right_ref)):
        again = halo_spare[side]
        extra = jnp.where(keep, jnp.concatenate([again, again], axis=0), 0.0)
        high, middle, _ = split3(jnp.concatenate([halo_pair[side], extra], axis=1))
        total = total + (dot_nt(ref[0], high) + (dot_nt(ref[0], middle) + dot_nt(ref[1], high)))
    out_ref[...] = total[:, 0:DATES]


def on_device(phases, pairs, class_weights, classes):
    own_ifg, tile_rows, cols = phases.shape
    tile_cols = classes.shape[1]
    pixels = tile_rows * tile_cols
    count = cols // tile_cols
    nifg = pairs.shape[0]
    half = pixels // 2
    vmem = pl.BlockSpec(memory_space=pltpu.VMEM)
    f32, bf16 = jnp.float32, jnp.bfloat16
    copies = 2 * CHUNKS + 5

    blocks = phases.transpose(0, 2, 1).reshape(own_ifg, count, pixels).transpose(1, 0, 2)
    padded = jnp.pad(class_weights, ((0, LANES - CLASSES), (0, 0)))
    corrected = pl.pallas_call(
        functools.partial(kernel, tile_rows, tile_cols),
        out_shape=jax.ShapeDtypeStruct((pixels, DATES), f32),
        in_specs=[vmem] * 5,
        out_specs=vmem,
        scratch_shapes=[
            pltpu.VMEM((count, own_ifg, pixels), f32),
            pltpu.VMEM((PAD, nifg), bf16),
            pltpu.VMEM((nifg, pixels), f32),
            pltpu.VMEM((MAXGAP + 1, PAD, pixels), f32),
            pltpu.VMEM((MAXGAP + 1, PAD, LANES), f32),
            pltpu.VMEM((MAXGAP + 1, PAD, LANES), f32),
            pltpu.VMEM((pixels, pixels), f32),
            pltpu.VMEM((2, pixels, pixels), bf16),
            pltpu.VMEM((2, pixels, pixels), bf16),
            pltpu.VMEM((16, pixels), f32),
            pltpu.VMEM((3, pixels, 16), f32),
            pltpu.VMEM((PAD + 8, pixels), f32),
            pltpu.VMEM((PAD, pixels), f32),
            pltpu.VMEM((2, PAD // 2, half), f32),
            pltpu.VMEM((16, PAD), f32),
            pltpu.VMEM((2, PAD, half), f32),
            pltpu.VMEM((2, PAD // 2, half), f32),
            pltpu.VMEM((3, 16, PAD), f32),
            pltpu.SemaphoreType.DMA((count,)),
            pltpu.SemaphoreType.DMA((count,)),
            pltpu.SemaphoreType.DMA,
            pltpu.SemaphoreType.DMA((copies,)),
            pltpu.SemaphoreType.DMA((copies,)),
        ],
        compiler_params=pltpu.CompilerParams(
            collective_id=0, has_side_effects=True, vmem_limit_bytes=48 * 1024 * 1024
        ),
        name="invert_and_filter",
    )(blocks, pairs.T, padded, padded.T, classes.T.reshape(1, pixels))
    return corrected.reshape(tile_rows, tile_cols, DATES)


def solution(mesh):
    return jax.shard_map(
        on_device,
        mesh=mesh,
        in_specs=(P("ifg", "tile", None), P(), P(), P("tile", "ifg")),
        out_specs=P("tile", "ifg", None),
        check_vma=False,
    )
```

```python
import functools
import math
import jax
import jax.numpy as jnp
from jax import lax
from jax.experimental import pallas as pl
from jax.experimental.pallas import tpu as pltpu
from jax.sharding import PartitionSpec as P

DATES = 300
CLASSES = 8
MAXGAP = 8
R = 3
LANES = 128
PAD = -(-DATES // 8) * 8
CHUNKS = (2, 4)
MESH = pl.DeviceIdType.MESH
HIGHEST = lax.Precision.HIGHEST

smooth_weight = 1.0
anchor_weight = 0.1


def split3(value):
    high = value.astype(jnp.bfloat16)
    rest = value - high.astype(jnp.float32)
    middle = rest.astype(jnp.bfloat16)
    low = (rest - middle.astype(jnp.float32)).astype(jnp.bfloat16)
    return (high, middle, low)


def dot_nt(a, b, **kw):
    return lax.dot_general(a, b, (((1,), (1,)), ((), ())), preferred_element_type=jnp.float32, **kw)


def dot_nn(a, b, **kw):
    return lax.dot_general(a, b, (((1,), (0,)), ((), ())), preferred_element_type=jnp.float32, **kw)


def factor(pairs_ref, w_ref, wt_ref, cls_ref, inc_ref, wpx_ref, lpx_ref, band, low):
    nifg = pairs_ref.shape[1]
    pixels = cls_ref.shape[1]
    first = pairs_ref[0:1, :]
    second = pairs_ref[1:2, :]
    gap = second - first
    dates = lax.broadcasted_iota(jnp.int32, (PAD, nifg), 0)
    minus_f = jnp.where(dates == first, 1.0, 0.0)
    plus_f = jnp.where(dates == second, 1.0, 0.0)
    inc_ref[...] = (plus_f - minus_f).astype(jnp.bfloat16)
    minus = minus_f.astype(jnp.bfloat16)
    both = (plus_f + minus_f).astype(jnp.bfloat16)
    w = w_ref[...]
    row = lax.broadcasted_iota(jnp.int32, (PAD, LANES), 0)
    inside = lambda ok: jnp.where(ok, 1.0, 0.0)
    for g in range(MAXGAP + 1):
        parts = split3(w if g == 0 else jnp.where(gap == g, w, 0.0))
        left = both if g == 0 else minus
        total = dot_nt(left, parts[0]) + (dot_nt(left, parts[1]) + dot_nt(left, parts[2]))
        here = inside(row <= DATES - 3)
        before = inside((row >= 1) & (row <= DATES - 2))
        if g == 0:
            twice = inside((row >= 2) & (row <= DATES - 1))
            prior = smooth_weight * (here + 4.0 * before + twice) + anchor_weight
            total = total + jnp.where(row < DATES, prior, 1.0)
        elif g == 1:
            total = smooth_weight * (-2.0 * here - 2.0 * before) - total
        elif g == 2:
            total = smooth_weight * here - total
        else:
            total = -total
        band[g] = total

    zero = jnp.zeros((1, LANES), jnp.float32)
    keys = [(j, h) for j in range(MAXGAP) for h in range(MAXGAP - j)]

    def factor_block(block, carry):
        acc = dict(zip(keys, carry))
        base = pl.multiple_of(block * 8, 8)
        for s in range(8):
            at = pl.ds(base + s, 1)
            c = [band[h, at, :] for h in range(MAXGAP + 1)]
            c = [c[h] - acc[(0, h)] for h in range(MAXGAP)] + [c[MAXGAP]]
            inv = 1.0 / c[0]
            low[0, at, :] = inv
            fresh = {}
            for j in range(1, MAXGAP + 1):
                lj = c[j] * inv
                low[j, at, :] = lj
                for h in range(MAXGAP - j + 1):
                    term = lj * c[j + h]
                    old = acc.get((j, h))
                    fresh[(j - 1, h)] = term if old is None else old + term
            acc = fresh
        return tuple(acc[k] for k in keys)

    lax.fori_loop(0, PAD // 8, factor_block, tuple(zero for _ in keys))

    member = lax.broadcasted_iota(jnp.int32, (LANES, pixels), 0)
    onehot = jnp.where(member == cls_ref[...], 1.0, 0.0).astype(jnp.bfloat16)

    def expand(value):
        parts = split3(value)
        return dot_nn(parts[0], onehot) + (dot_nn(parts[1], onehot) + dot_nn(parts[2], onehot))

    for g in range(MAXGAP + 1):
        value = expand(low[g])
        lpx_ref[0, g] = value[:, 0:pixels // 2]
        lpx_ref[1, g] = value[:, pixels // 2:]
    wpx_ref[...] = expand(wt_ref[...])


NORM = sum(math.exp(-j * j / 4.5) for j in range(-R, R + 1))


def tap(delta):
    near = jnp.exp((delta * delta).astype(jnp.float32) * (-1.0 / 4.5)) * (1.0 / NORM)
    return jnp.where(jnp.abs(delta) <= R, near, 0.0)


def split_index(index, size):
    if size & (size - 1):
        return index // size, index % size
    return index >> (size.bit_length() - 1), index & (size - 1)


def iota(shape, dim):
    return lax.broadcasted_iota(jnp.int32, shape, dim)


def fill_filters(tile_rows, tile_cols, own_ref, left_ref, right_ref, sel_ref, tile_ref):
    pixels = tile_rows * tile_cols
    me, core = lax.axis_index("ifg"), lax.axis_index("tile")
    count = lax.axis_size("ifg")
    has_left = jnp.where(me > 0, 1.0, 0.0)
    has_right = jnp.where(me < count - 1, 1.0, 0.0)
    square = (pixels, pixels)
    out_r, out_c = split_index(iota(square, 0), tile_cols)
    in_c, in_r = split_index(iota(square, 1), tile_rows)
    vertical = tap(out_r - in_r)
    same = jnp.where((out_r == in_r) & (out_c == in_c), 1.0, 0.0)
    own_ref[...] = same - vertical * tap(out_c - in_c)
    from_left = jnp.where(in_c >= 2, 1, in_c + 2)
    from_right = jnp.where(in_c >= 2, 2, in_c)
    left = -has_left * vertical * tap(out_c - from_left + tile_cols)
    right = -has_right * vertical * tap(out_c - from_right - tile_cols)
    for ref, value in ((left_ref, left), (right_ref, right)):
        parts = split3(value)
        ref[0] = parts[0]
        ref[1] = parts[1]
    slot_c, slot_j = split_index(iota((16, pixels), 0), 4)
    sel_c, sel_r = split_index(iota((16, pixels), 1), tile_rows)
    sent_r = jnp.where(core == 0, tile_rows - R, 0) + slot_j
    sel_ref[...] = jnp.where((slot_j < R) & (sent_r == sel_r) & (slot_c == sel_c), 1.0, 0.0)
    slot_c, slot_j = split_index(iota((pixels, 16), 1), 4)
    out_r, out_c = split_index(iota((pixels, 16), 0), tile_cols)
    got_r = jnp.where(core == 0, tile_rows, -R) + slot_j
    reach = jnp.where(slot_j < R, tap(out_r - got_r), 0.0)
    tile_ref[0] = -has_left * reach * tap(out_c - slot_c + tile_cols)
    tile_ref[1] = -reach * tap(out_c - slot_c)
    tile_ref[2] = -has_right * reach * tap(out_c - slot_c - tile_cols)


def kernel(tile_rows, tile_cols, blocks_ref, pairs_ref, w_ref, wt_ref, cls_ref, out_ref,
           recv, inc_ref, wpx_ref, lpx_ref, band, low, own_ref, left_ref, right_ref, sel_ref,
           tile_ref, rows, x_ref, spare, edge, halo_pair, halo_spare, halo_tile,
           all_send, all_recv, own_sem, send_sem, recv_sem):
    me = lax.axis_index("ifg")
    core = lax.axis_index("tile")
    count = lax.axis_size("ifg")
    left = lax.rem(me + count - 1, count)
    right = lax.rem(me + 1, count)
    other = 1 - core
    near = [(me, other), (left, other), (right, other)]
    barrier = pltpu.get_barrier_semaphore()

    def greet(k, _):
        pl.semaphore_signal(barrier, inc=1, device_id=(lax.rem(me + k, count), core), device_id_type=MESH)
        return _

    lax.fori_loop(1, count, greet, 0)
    for partner in near:
        pl.semaphore_signal(barrier, inc=1, device_id=partner, device_id_type=MESH)
    pl.semaphore_wait(barrier, count - 1 + len(near))

    def exchange(part, k, slot):
        peer = lax.rem(me + k, count)
        return pltpu.make_async_remote_copy(
            src_ref=blocks_ref.at[part, peer], dst_ref=recv.at[part, slot],
            send_sem=all_send.at[part, k], recv_sem=all_recv.at[part, k],
            device_id=(peer, core), device_id_type=MESH)

    def own_copy(part):
        return pltpu.make_async_copy(blocks_ref.at[part, me], recv.at[part, me], own_sem.at[part])

    for part in range(2):
        def send_block(k, _, part=part):
            exchange(part, k, me).start()
            return _

        lax.fori_loop(1, count, send_block, 0)
        own_copy(part).start()

    factor(pairs_ref, w_ref, wt_ref, cls_ref, inc_ref, wpx_ref, lpx_ref, band, low)

    def copy(i, src, dst, device):
        return pltpu.make_async_remote_copy(src_ref=src, dst_ref=dst, send_sem=send_sem.at[i],
                                            recv_sem=recv_sem.at[i], device_id=device,
                                            device_id_type=MESH)

    half = x_ref.shape[2]
    mid = PAD // 2
    low_lanes = iota((mid, half), 1) < half // 2
    rows[PAD:PAD + 8, :] = jnp.zeros((8, half), jnp.float32)
    sent = ([], [])
    at_copy = 0
    for part in range(2):
        lanes = pl.ds(part * half, half)

        def take_block(k, _, part=part):
            exchange(part, k, lax.rem(me + count - k, count)).wait()
            return _

        own_copy(part).wait()
        lax.fori_loop(1, count, take_block, 0)
        high, middle, _ = split3(recv[part].reshape(-1, half) * wpx_ref[:, lanes])
        both = dot_nn(inc_ref[...], jnp.concatenate([high, middle], axis=1))
        rows[0:PAD, :] = both[:, 0:half] + both[:, half:]

        def forward(block, carry, part=part):
            a = list(carry)
            base = pl.multiple_of(block * 8, 8)
            for s in range(8):
                at = pl.ds(base + s, 1)
                y = a[0]
                a = a[1:] + [rows[pl.ds(base + s + 8, 1), :]]
                a = [a[j] - lpx_ref[part, j + 1, at, :] * y for j in range(8)]
                x_ref[part, at, :] = y * lpx_ref[part, 0, at, :]
            return tuple(a)

        lax.fori_loop(0, PAD // 8, forward, tuple(rows[d:d + 1, :] for d in range(8)))

        def backward(block, carry, part=part):
            later = list(carry)
            base = pl.multiple_of(block * 8, 8)
            for s in range(7, -1, -1):
                at = pl.ds(base + s, 1)
                value = x_ref[part, at, :]
                for g in range(8, 0, -1):
                    value = value - lpx_ref[part, g, at, :] * later[g - 1]
                x_ref[part, at, :] = value
                later = [value] + later[:7]
            return tuple(later)

        toward, back = ((left, core), (right, core)) if part == 0 else ((right, core), (left, core))
        blocks = PAD // 8
        chunks = CHUNKS[part]
        cuts = [blocks * (chunks - i) // chunks for i in range(chunks + 1)]
        carry = tuple(jnp.zeros((1, half), jnp.float32) for _ in range(8))
        for top, bottom in zip(cuts[:-1], cuts[1:]):
            carry = lax.fori_loop(0, top - bottom, lambda n, c, top=top, run=backward: run(top - 1 - n, c), carry)
            span = pl.ds(bottom * 8, (top - bottom) * 8)
            sent[1 - part].append(copy(at_copy, x_ref.at[part, span], halo_pair.at[1 - part, span], toward))
            sent[1 - part][-1].start()
            at_copy += 1
        piece = x_ref[part]
        if part == 0:
            spare[0] = jnp.where(low_lanes, pltpu.roll(piece[0:mid], half // 2, 1), piece[mid:])
        else:
            spare[1] = jnp.where(low_lanes, piece[0:mid], pltpu.roll(piece[mid:], half // 2, 1))
        sent[part].append(copy(at_copy, spare.at[part], halo_spare.at[part], back))
        sent[part][-1].start()
        at_copy += 1
        if part == 0:
            fill_filters(tile_rows, tile_cols, own_ref, left_ref, right_ref, sel_ref, tile_ref)
    x = jnp.concatenate([x_ref[0], x_ref[1]], axis=1)
    edge[...] = dot_nt(sel_ref[...], x, precision=HIGHEST)
    small = [copy(at_copy + i, edge, halo_tile.at[slot], near[i]) for i, slot in enumerate((1, 2, 0))]
    for c in small:
        c.start()
    total = dot_nt(own_ref[...], x, precision=HIGHEST)
    for c in small:
        c.wait()
    for i in range(3):
        total += dot_nn(tile_ref[i], halo_tile[i], precision=HIGHEST)
    keep = (iota((PAD, half), 0) < mid) == (iota((PAD, half), 1) < half // 2)
    for side, ref in ((1, right_ref), (0, left_ref)):
        for c in sent[side]:
            c.wait()
        again = halo_spare[side]
        extra = jnp.where(keep, jnp.concatenate([again, again], axis=0), 0.0)
        high, middle, _ = split3(jnp.concatenate([halo_pair[side], extra], axis=1))
        total = total + (dot_nt(ref[0], high) + (dot_nt(ref[0], middle) + dot_nt(ref[1], high)))
    out_ref[...] = total[:, 0:DATES]


def on_device(phases, pairs, class_weights, classes):
    own_ifg, tile_rows, cols = phases.shape
    tile_cols = classes.shape[1]
    pixels = tile_rows * tile_cols
    count = cols // tile_cols
    nifg = pairs.shape[0]
    half = pixels // 2
    vmem = pl.BlockSpec(memory_space=pltpu.VMEM)
    f32, bf16 = jnp.float32, jnp.bfloat16
    copies = sum(CHUNKS) + 5

    blocks = phases.transpose(0, 2, 1).reshape(own_ifg, count, 2, half).transpose(2, 1, 0, 3)
    padded = jnp.pad(class_weights, ((0, LANES - CLASSES), (0, 0)))
    corrected = pl.pallas_call(
        functools.partial(kernel, tile_rows, tile_cols),
        out_shape=jax.ShapeDtypeStruct((pixels, DATES), f32),
        in_specs=[vmem] * 5,
        out_specs=vmem,
        scratch_shapes=[
            pltpu.VMEM((2, count, own_ifg, half), f32),
            pltpu.VMEM((PAD, nifg), bf16),
            pltpu.VMEM((nifg, pixels), f32),
            pltpu.VMEM((2, MAXGAP + 1, PAD, half), f32),
            pltpu.VMEM((MAXGAP + 1, PAD, LANES), f32),
            pltpu.VMEM((MAXGAP + 1, PAD, LANES), f32),
            pltpu.VMEM((pixels, pixels), f32),
            pltpu.VMEM((2, pixels, pixels), bf16),
            pltpu.VMEM((2, pixels, pixels), bf16),
            pltpu.VMEM((16, pixels), f32),
            pltpu.VMEM((3, pixels, 16), f32),
            pltpu.VMEM((PAD + 8, half), f32),
            pltpu.VMEM((2, PAD, half), f32),
            pltpu.VMEM((2, PAD // 2, half), f32),
            pltpu.VMEM((16, PAD), f32),
            pltpu.VMEM((2, PAD, half), f32),
            pltpu.VMEM((2, PAD // 2, half), f32),
            pltpu.VMEM((3, 16, PAD), f32),
            pltpu.SemaphoreType.DMA((2, count)),
            pltpu.SemaphoreType.DMA((2, count)),
            pltpu.SemaphoreType.DMA((2,)),
            pltpu.SemaphoreType.DMA((copies,)),
            pltpu.SemaphoreType.DMA((copies,)),
        ],
        compiler_params=pltpu.CompilerParams(
            collective_id=0, has_side_effects=True, vmem_limit_bytes=48 * 1024 * 1024
        ),
        name="invert_and_filter",
    )(blocks, pairs.T, padded, padded.T, classes.T.reshape(1, pixels))
    return corrected.reshape(tile_rows, tile_cols, DATES)


def solution(mesh):
    return jax.shard_map(
        on_device,
        mesh=mesh,
        in_specs=(P("ifg", "tile", None), P(), P(), P("tile", "ifg")),
        out_specs=P("tile", "ifg", None),
        check_vma=False,
    )
```

```python
import functools
import math
import jax
import jax.numpy as jnp
from jax import lax
from jax.experimental import pallas as pl
from jax.experimental.pallas import tpu as pltpu
from jax.sharding import PartitionSpec as P

DATES = 300
CLASSES = 8
MAXGAP = 8
R = 3
LANES = 128
PAD = -(-DATES // 8) * 8
CHUNKS = 4
MESH = pl.DeviceIdType.MESH
HIGHEST = lax.Precision.HIGHEST

smooth_weight = 1.0
anchor_weight = 0.1


def split3(value):
    high = value.astype(jnp.bfloat16)
    rest = value - high.astype(jnp.float32)
    middle = rest.astype(jnp.bfloat16)
    low = (rest - middle.astype(jnp.float32)).astype(jnp.bfloat16)
    return (high, middle, low)


def dot_nt(a, b, **kw):
    return lax.dot_general(a, b, (((1,), (1,)), ((), ())), preferred_element_type=jnp.float32, **kw)


def dot_nn(a, b, **kw):
    return lax.dot_general(a, b, (((1,), (0,)), ((), ())), preferred_element_type=jnp.float32, **kw)


def factor(pairs_ref, w_ref, wt_ref, cls_ref, inc_ref, wpx_ref, lpx_ref, band, low):
    nifg = pairs_ref.shape[1]
    pixels = cls_ref.shape[1]
    first = pairs_ref[0:1, :]
    second = pairs_ref[1:2, :]
    gap = second - first
    dates = lax.broadcasted_iota(jnp.int32, (PAD, nifg), 0)
    minus_f = jnp.where(dates == first, 1.0, 0.0)
    plus_f = jnp.where(dates == second, 1.0, 0.0)
    inc_ref[...] = (plus_f - minus_f).astype(jnp.bfloat16)
    minus = minus_f.astype(jnp.bfloat16)
    both = (plus_f + minus_f).astype(jnp.bfloat16)
    w = w_ref[...]
    row = lax.broadcasted_iota(jnp.int32, (PAD, LANES), 0)
    inside = lambda ok: jnp.where(ok, 1.0, 0.0)
    for g in range(MAXGAP + 1):
        parts = split3(w if g == 0 else jnp.where(gap == g, w, 0.0))
        left = both if g == 0 else minus
        total = dot_nt(left, parts[0]) + (dot_nt(left, parts[1]) + dot_nt(left, parts[2]))
        here = inside(row <= DATES - 3)
        before = inside((row >= 1) & (row <= DATES - 2))
        if g == 0:
            twice = inside((row >= 2) & (row <= DATES - 1))
            prior = smooth_weight * (here + 4.0 * before + twice) + anchor_weight
            total = total + jnp.where(row < DATES, prior, 1.0)
        elif g == 1:
            total = smooth_weight * (-2.0 * here - 2.0 * before) - total
        elif g == 2:
            total = smooth_weight * here - total
        else:
            total = -total
        band[g] = total

    zero = jnp.zeros((1, LANES), jnp.float32)
    keys = [(j, h) for j in range(MAXGAP) for h in range(MAXGAP - j)]

    def factor_block(block, carry):
        acc = dict(zip(keys, carry))
        base = pl.multiple_of(block * 8, 8)
        for s in range(8):
            at = pl.ds(base + s, 1)
            c = [band[h, at, :] for h in range(MAXGAP + 1)]
            c = [c[h] - acc[(0, h)] for h in range(MAXGAP)] + [c[MAXGAP]]
            inv = 1.0 / c[0]
            low[0, at, :] = inv
            fresh = {}
            for j in range(1, MAXGAP + 1):
                lj = c[j] * inv
                low[j, at, :] = lj
                for h in range(MAXGAP - j + 1):
                    term = lj * c[j + h]
                    old = acc.get((j, h))
                    fresh[(j - 1, h)] = term if old is None else old + term
            acc = fresh
        return tuple(acc[k] for k in keys)

    lax.fori_loop(0, PAD // 8, factor_block, tuple(zero for _ in keys))

    member = lax.broadcasted_iota(jnp.int32, (LANES, pixels), 0)
    onehot = jnp.where(member == cls_ref[...], 1.0, 0.0).astype(jnp.bfloat16)

    def expand(value):
        parts = split3(value)
        return dot_nn(parts[0], onehot) + (dot_nn(parts[1], onehot) + dot_nn(parts[2], onehot))

    for g in range(MAXGAP + 1):
        lpx_ref[g] = expand(low[g])
    wpx_ref[...] = expand(wt_ref[...])


NORM = sum(math.exp(-j * j / 4.5) for j in range(-R, R + 1))


def tap(delta):
    near = jnp.exp((delta * delta).astype(jnp.float32) * (-1.0 / 4.5)) * (1.0 / NORM)
    return jnp.where(jnp.abs(delta) <= R, near, 0.0)


def split_index(index, size):
    if size & (size - 1):
        return index // size, index % size
    return index >> (size.bit_length() - 1), index & (size - 1)


def iota(shape, dim):
    return lax.broadcasted_iota(jnp.int32, shape, dim)


def fill_filters(tile_rows, tile_cols, own_ref, left_ref, right_ref, sel_ref, tile_ref):
    pixels = tile_rows * tile_cols
    me, core = lax.axis_index("ifg"), lax.axis_index("tile")
    count = lax.axis_size("ifg")
    has_left = jnp.where(me > 0, 1.0, 0.0)
    has_right = jnp.where(me < count - 1, 1.0, 0.0)
    square = (pixels, pixels)
    out_r, out_c = split_index(iota(square, 0), tile_cols)
    in_c, in_r = split_index(iota(square, 1), tile_rows)
    vertical = tap(out_r - in_r)
    same = jnp.where((out_r == in_r) & (out_c == in_c), 1.0, 0.0)
    own_ref[...] = same - vertical * tap(out_c - in_c)
    from_left = jnp.where(in_c >= 2, 1, in_c + 2)
    from_right = jnp.where(in_c >= 2, 2, in_c)
    left = -has_left * vertical * tap(out_c - from_left + tile_cols)
    right = -has_right * vertical * tap(out_c - from_right - tile_cols)
    for ref, value in ((left_ref, left), (right_ref, right)):
        parts = split3(value)
        ref[0] = parts[0]
        ref[1] = parts[1]
    slot_c, slot_j = split_index(iota((16, pixels), 0), 4)
    sel_c, sel_r = split_index(iota((16, pixels), 1), tile_rows)
    sent_r = jnp.where(core == 0, tile_rows - R, 0) + slot_j
    sel_ref[...] = jnp.where((slot_j < R) & (sent_r == sel_r) & (slot_c == sel_c), 1.0, 0.0)
    slot_c, slot_j = split_index(iota((pixels, 16), 1), 4)
    out_r, out_c = split_index(iota((pixels, 16), 0), tile_cols)
    got_r = jnp.where(core == 0, tile_rows, -R) + slot_j
    reach = jnp.where(slot_j < R, tap(out_r - got_r), 0.0)
    tile_ref[0] = -has_left * reach * tap(out_c - slot_c + tile_cols)
    tile_ref[1] = -reach * tap(out_c - slot_c)
    tile_ref[2] = -has_right * reach * tap(out_c - slot_c - tile_cols)


def kernel(tile_rows, tile_cols, blocks_ref, pairs_ref, w_ref, wt_ref, cls_ref, out_ref,
           recv, inc_ref, wpx_ref, lpx_ref, band, low, own_ref, left_ref, right_ref, sel_ref,
           tile_ref, rows, x_ref, spare, edge, halo_pair, halo_spare, halo_tile,
           all_send, all_recv, own_sem, send_sem, recv_sem):
    me = lax.axis_index("ifg")
    core = lax.axis_index("tile")
    count = lax.axis_size("ifg")
    left = lax.rem(me + count - 1, count)
    right = lax.rem(me + 1, count)
    other = 1 - core
    near = [(me, other), (left, other), (right, other)]
    barrier = pltpu.get_barrier_semaphore()

    def greet(k, _):
        pl.semaphore_signal(barrier, inc=1, device_id=(lax.rem(me + k, count), core), device_id_type=MESH)
        return _

    lax.fori_loop(1, count, greet, 0)
    for partner in near:
        pl.semaphore_signal(barrier, inc=1, device_id=partner, device_id_type=MESH)
    pl.semaphore_wait(barrier, count - 1 + len(near))

    def exchange(k, slot):
        peer = lax.rem(me + k, count)
        return pltpu.make_async_remote_copy(
            src_ref=blocks_ref.at[peer], dst_ref=recv.at[slot], send_sem=all_send.at[k],
            recv_sem=all_recv.at[k], device_id=(peer, core), device_id_type=MESH)

    def send_block(k, _):
        exchange(k, me).start()
        return _

    lax.fori_loop(1, count, send_block, 0)
    mine = pltpu.make_async_copy(blocks_ref.at[me], recv.at[me], own_sem)
    mine.start()

    factor(pairs_ref, w_ref, wt_ref, cls_ref, inc_ref, wpx_ref, lpx_ref, band, low)
    fill_filters(tile_rows, tile_cols, own_ref, left_ref, right_ref, sel_ref, tile_ref)

    def take_block(k, _):
        exchange(k, lax.rem(me + count - k, count)).wait()
        return _

    mine.wait()
    lax.fori_loop(1, count, take_block, 0)

    pixels = x_ref.shape[1]
    parts = split3(recv[...].reshape(-1, pixels) * wpx_ref[...])
    inc = inc_ref[...]
    rows[0:PAD, :] = dot_nn(inc, parts[0]) + dot_nn(inc, parts[1])
    rows[PAD:PAD + 8, :] = jnp.zeros((8, pixels), jnp.float32)

    def forward(block, carry):
        a = list(carry)
        base = pl.multiple_of(block * 8, 8)
        for s in range(8):
            at = pl.ds(base + s, 1)
            y = a[0]
            a = a[1:] + [rows[pl.ds(base + s + 8, 1), :]]
            a = [a[j] - lpx_ref[j + 1, at, :] * y for j in range(8)]
            x_ref[at, :] = y * lpx_ref[0, at, :]
        return tuple(a)

    lax.fori_loop(0, PAD // 8, forward, tuple(rows[d:d + 1, :] for d in range(8)))

    def backward(block, carry):
        later = list(carry)
        base = pl.multiple_of(block * 8, 8)
        for s in range(7, -1, -1):
            at = pl.ds(base + s, 1)
            value = x_ref[at, :]
            for g in range(8, 0, -1):
                value = value - lpx_ref[g, at, :] * later[g - 1]
            x_ref[at, :] = value
            later = [value] + later[:7]
        return tuple(later)

    def copy(i, src, dst, device):
        return pltpu.make_async_remote_copy(src_ref=src, dst_ref=dst, send_sem=send_sem.at[i],
                                            recv_sem=recv_sem.at[i], device_id=device,
                                            device_id_type=MESH)

    has_left, has_right = me > 0, me < count - 1

    @pl.when(jnp.logical_not(has_left))
    def _():
        halo_pair[0] = jnp.zeros_like(halo_pair[0])
        halo_spare[0] = jnp.zeros_like(halo_spare[0])
        halo_tile[0] = jnp.zeros_like(halo_tile[0])

    @pl.when(jnp.logical_not(has_right))
    def _():
        halo_pair[1] = jnp.zeros_like(halo_pair[1])
        halo_spare[1] = jnp.zeros_like(halo_spare[1])
        halo_tile[2] = jnp.zeros_like(halo_tile[2])

    half = pixels // 2
    total_blocks = PAD // 8
    cuts = [total_blocks * (CHUNKS - i) // CHUNKS for i in range(CHUNKS + 1)]
    carry = tuple(jnp.zeros((1, pixels), jnp.float32) for _ in range(8))
    to_left, to_right = [], []
    for i in range(CHUNKS):
        top, bottom = cuts[i], cuts[i + 1]
        carry = lax.fori_loop(0, top - bottom, lambda n, c, top=top: backward(top - 1 - n, c), carry)
        span = pl.ds(bottom * 8, (top - bottom) * 8)
        to_left.append(copy(2 * i, x_ref.at[span, pl.ds(0, half)], halo_pair.at[1, span], (left, core)))
        to_right.append(copy(2 * i + 1, x_ref.at[span, pl.ds(half, half)], halo_pair.at[0, span], (right, core)))
        if i < CHUNKS - 1:
            pl.when(has_left)(to_left[-1].start)
            pl.when(has_right)(to_right[-1].start)
    x = x_ref[...]
    edge[...] = dot_nt(sel_ref[...], x, precision=HIGHEST)
    small = [copy(2 * CHUNKS + 2 + i, edge, halo_tile.at[slot], near[i]) for i, slot in enumerate((1, 2, 0))]
    small[0].start()
    pl.when(has_left)(small[1].start)
    pl.when(has_right)(small[2].start)
    pl.when(has_left)(to_left[-1].start)
    pl.when(has_right)(to_right[-1].start)
    mid = PAD // 2
    low_lanes = iota((mid, half), 1) < half // 2
    first, second = x[:, 0:half], x[:, half:]
    spare[0] = jnp.where(low_lanes, pltpu.roll(first[0:mid], half // 2, 1), first[mid:])
    spare[1] = jnp.where(low_lanes, second[0:mid], pltpu.roll(second[mid:], half // 2, 1))
    to_right.append(copy(2 * CHUNKS, spare.at[0], halo_spare.at[0], (right, core)))
    to_left.append(copy(2 * CHUNKS + 1, spare.at[1], halo_spare.at[1], (left, core)))
    pl.when(has_right)(to_right[-1].start)
    pl.when(has_left)(to_left[-1].start)
    total = dot_nt(own_ref[...], x, precision=HIGHEST)
    small[0].wait()
    pl.when(has_left)(small[1].wait_send)
    pl.when(has_right)(small[1].wait_recv)
    pl.when(has_right)(small[2].wait_send)
    pl.when(has_left)(small[2].wait_recv)
    for i in range(3):
        total += dot_nn(tile_ref[i], halo_tile[i], precision=HIGHEST)
    for c in to_right:
        pl.when(has_right)(c.wait_send)
        pl.when(has_left)(c.wait_recv)
    for c in to_left:
        pl.when(has_left)(c.wait_send)
        pl.when(has_right)(c.wait_recv)
    keep = (iota((PAD, half), 0) < mid) == (iota((PAD, half), 1) < half // 2)
    for side, ref in ((0, left_ref), (1, right_ref)):
        again = halo_spare[side]
        extra = jnp.where(keep, jnp.concatenate([again, again], axis=0), 0.0)
        high, middle, _ = split3(jnp.concatenate([halo_pair[side], extra], axis=1))
        total = total + (dot_nt(ref[0], high) + (dot_nt(ref[0], middle) + dot_nt(ref[1], high)))
    out_ref[...] = total[:, 0:DATES]


def on_device(phases, pairs, class_weights, classes):
    own_ifg, tile_rows, cols = phases.shape
    tile_cols = classes.shape[1]
    pixels = tile_rows * tile_cols
    count = cols // tile_cols
    nifg = pairs.shape[0]
    half = pixels // 2
    vmem = pl.BlockSpec(memory_space=pltpu.VMEM)
    f32, bf16 = jnp.float32, jnp.bfloat16
    copies = 2 * CHUNKS + 5

    blocks = phases.transpose(0, 2, 1).reshape(own_ifg, count, pixels).transpose(1, 0, 2)
    padded = jnp.pad(class_weights, ((0, LANES - CLASSES), (0, 0)))
    corrected = pl.pallas_call(
        functools.partial(kernel, tile_rows, tile_cols),
        out_shape=jax.ShapeDtypeStruct((pixels, DATES), f32),
        in_specs=[vmem] * 5,
        out_specs=vmem,
        scratch_shapes=[
            pltpu.VMEM((count, own_ifg, pixels), f32),
            pltpu.VMEM((PAD, nifg), bf16),
            pltpu.VMEM((nifg, pixels), f32),
            pltpu.VMEM((MAXGAP + 1, PAD, pixels), f32),
            pltpu.VMEM((MAXGAP + 1, PAD, LANES), f32),
            pltpu.VMEM((MAXGAP + 1, PAD, LANES), f32),
            pltpu.VMEM((pixels, pixels), f32),
            pltpu.VMEM((2, pixels, pixels), bf16),
            pltpu.VMEM((2, pixels, pixels), bf16),
            pltpu.VMEM((16, pixels), f32),
            pltpu.VMEM((3, pixels, 16), f32),
            pltpu.VMEM((PAD + 8, pixels), f32),
            pltpu.VMEM((PAD, pixels), f32),
            pltpu.VMEM((2, PAD // 2, half), f32),
            pltpu.VMEM((16, PAD), f32),
            pltpu.VMEM((2, PAD, half), f32),
            pltpu.VMEM((2, PAD // 2, half), f32),
            pltpu.VMEM((3, 16, PAD), f32),
            pltpu.SemaphoreType.DMA((count,)),
            pltpu.SemaphoreType.DMA((count,)),
            pltpu.SemaphoreType.DMA,
            pltpu.SemaphoreType.DMA((copies,)),
            pltpu.SemaphoreType.DMA((copies,)),
        ],
        compiler_params=pltpu.CompilerParams(
            collective_id=0, has_side_effects=True, vmem_limit_bytes=48 * 1024 * 1024
        ),
        name="invert_and_filter",
    )(blocks, pairs.T, padded, padded.T, classes.T.reshape(1, pixels))
    return corrected.reshape(tile_rows, tile_cols, DATES)


def solution(mesh):
    return jax.shard_map(
        on_device,
        mesh=mesh,
        in_specs=(P("ifg", "tile", None), P(), P(), P("tile", "ifg")),
        out_specs=P("tile", "ifg", None),
        check_vma=False,
    )
```

```python
import functools
import math
import jax
import jax.numpy as jnp
from jax import lax
from jax.experimental import pallas as pl
from jax.experimental.pallas import tpu as pltpu
from jax.sharding import PartitionSpec as P

DATES = 300
CLASSES = 8
MAXGAP = 8
R = 3
LANES = 128
PAD = -(-DATES // 8) * 8
CHUNKS = 4
MESH = pl.DeviceIdType.MESH
HIGHEST = lax.Precision.HIGHEST

smooth_weight = 1.0
anchor_weight = 0.1


def split3(value):
    high = value.astype(jnp.bfloat16)
    rest = value - high.astype(jnp.float32)
    middle = rest.astype(jnp.bfloat16)
    low = (rest - middle.astype(jnp.float32)).astype(jnp.bfloat16)
    return (high, middle, low)


def dot_nt(a, b, **kw):
    return lax.dot_general(a, b, (((1,), (1,)), ((), ())), preferred_element_type=jnp.float32, **kw)


def dot_nn(a, b, **kw):
    return lax.dot_general(a, b, (((1,), (0,)), ((), ())), preferred_element_type=jnp.float32, **kw)


def factor(pairs_ref, w_ref, wt_ref, cls_ref, inc_ref, wpx_ref, lpx_ref, band, low):
    nifg = pairs_ref.shape[1]
    pixels = cls_ref.shape[1]
    first = pairs_ref[0:1, :]
    second = pairs_ref[1:2, :]
    gap = second - first
    dates = lax.broadcasted_iota(jnp.int32, (PAD, nifg), 0)
    minus_f = jnp.where(dates == first, 1.0, 0.0)
    plus_f = jnp.where(dates == second, 1.0, 0.0)
    inc_ref[...] = (plus_f - minus_f).astype(jnp.bfloat16)
    minus = minus_f.astype(jnp.bfloat16)
    both = (plus_f + minus_f).astype(jnp.bfloat16)
    w = w_ref[...]
    row = lax.broadcasted_iota(jnp.int32, (PAD, LANES), 0)
    inside = lambda ok: jnp.where(ok, 1.0, 0.0)
    for g in range(MAXGAP + 1):
        parts = split3(w if g == 0 else jnp.where(gap == g, w, 0.0))
        left = both if g == 0 else minus
        total = dot_nt(left, parts[0]) + (dot_nt(left, parts[1]) + dot_nt(left, parts[2]))
        here = inside(row <= DATES - 3)
        before = inside((row >= 1) & (row <= DATES - 2))
        if g == 0:
            twice = inside((row >= 2) & (row <= DATES - 1))
            prior = smooth_weight * (here + 4.0 * before + twice) + anchor_weight
            total = total + jnp.where(row < DATES, prior, 1.0)
        elif g == 1:
            total = smooth_weight * (-2.0 * here - 2.0 * before) - total
        elif g == 2:
            total = smooth_weight * here - total
        else:
            total = -total
        band[g] = total

    zero = jnp.zeros((1, LANES), jnp.float32)
    keys = [(j, h) for j in range(MAXGAP) for h in range(MAXGAP - j)]

    def factor_block(block, carry):
        acc = dict(zip(keys, carry))
        base = pl.multiple_of(block * 8, 8)
        for s in range(8):
            at = pl.ds(base + s, 1)
            c = [band[h, at, :] for h in range(MAXGAP + 1)]
            c = [c[h] - acc[(0, h)] for h in range(MAXGAP)] + [c[MAXGAP]]
            inv = 1.0 / c[0]
            low[0, at, :] = inv
            fresh = {}
            for j in range(1, MAXGAP + 1):
                lj = c[j] * inv
                low[j, at, :] = lj
                for h in range(MAXGAP - j + 1):
                    term = lj * c[j + h]
                    old = acc.get((j, h))
                    fresh[(j - 1, h)] = term if old is None else old + term
            acc = fresh
        return tuple(acc[k] for k in keys)

    lax.fori_loop(0, PAD // 8, factor_block, tuple(zero for _ in keys))

    member = lax.broadcasted_iota(jnp.int32, (LANES, pixels), 0)
    onehot = jnp.where(member == cls_ref[...], 1.0, 0.0).astype(jnp.bfloat16)

    def expand(value):
        parts = split3(value)
        return dot_nn(parts[0], onehot) + (dot_nn(parts[1], onehot) + dot_nn(parts[2], onehot))

    for g in range(MAXGAP + 1):
        lpx_ref[g] = expand(low[g])
    wpx_ref[...] = expand(wt_ref[...])


NORM = sum(math.exp(-j * j / 4.5) for j in range(-R, R + 1))


def tap(delta):
    near = jnp.exp((delta * delta).astype(jnp.float32) * (-1.0 / 4.5)) * (1.0 / NORM)
    return jnp.where(jnp.abs(delta) <= R, near, 0.0)


def split_index(index, size):
    if size & (size - 1):
        return index // size, index % size
    return index >> (size.bit_length() - 1), index & (size - 1)


def iota(shape, dim):
    return lax.broadcasted_iota(jnp.int32, shape, dim)


def fill_filters(tile_rows, tile_cols, own_ref, left_ref, right_ref, sel_ref, tile_ref):
    pixels = tile_rows * tile_cols
    me, core = lax.axis_index("ifg"), lax.axis_index("tile")
    count = lax.axis_size("ifg")
    has_left = jnp.where(me > 0, 1.0, 0.0)
    has_right = jnp.where(me < count - 1, 1.0, 0.0)
    square = (pixels, pixels)
    out_r, out_c = split_index(iota(square, 0), tile_cols)
    in_c, in_r = split_index(iota(square, 1), tile_rows)
    vertical = tap(out_r - in_r)
    same = jnp.where((out_r == in_r) & (out_c == in_c), 1.0, 0.0)
    own_ref[...] = same - vertical * tap(out_c - in_c)
    from_left = jnp.where(in_c >= 2, 1, in_c + 2)
    from_right = jnp.where(in_c >= 2, 2, in_c)
    left = -has_left * vertical * tap(out_c - from_left + tile_cols)
    right = -has_right * vertical * tap(out_c - from_right - tile_cols)
    for ref, value in ((left_ref, left), (right_ref, right)):
        parts = split3(value)
        ref[0] = parts[0]
        ref[1] = parts[1]
    slot_c, slot_j = split_index(iota((16, pixels), 0), 4)
    sel_c, sel_r = split_index(iota((16, pixels), 1), tile_rows)
    sent_r = jnp.where(core == 0, tile_rows - R, 0) + slot_j
    sel_ref[...] = jnp.where((slot_j < R) & (sent_r == sel_r) & (slot_c == sel_c), 1.0, 0.0)
    side, slot = split_index(iota((pixels, 48), 1), 16)
    slot_c, slot_j = split_index(slot, 4)
    out_r, out_c = split_index(iota((pixels, 48), 0), tile_cols)
    got_r = jnp.where(core == 0, tile_rows, -R) + slot_j
    reach = jnp.where(slot_j < R, tap(out_r - got_r), 0.0)
    has = jnp.where(side == 0, has_left, jnp.where(side == 1, 1.0, has_right))
    tile_ref[...] = -has * reach * tap(out_c - slot_c + (1 - side) * tile_cols)


def kernel(tile_rows, tile_cols, blocks_ref, pairs_ref, w_ref, wt_ref, cls_ref, out_ref,
           recv, inc_ref, wpx_ref, lpx_ref, band, low, own_ref, left_ref, right_ref, sel_ref,
           tile_ref, rows, x_ref, spare, edge, halo_pair, halo_spare, halo_tile,
           all_send, all_recv, own_sem, send_sem, recv_sem):
    me = lax.axis_index("ifg")
    core = lax.axis_index("tile")
    count = lax.axis_size("ifg")
    left = lax.rem(me + count - 1, count)
    right = lax.rem(me + 1, count)
    other = 1 - core
    near = [(me, other), (left, other), (right, other)]
    barrier = pltpu.get_barrier_semaphore()

    def greet(k, _):
        pl.semaphore_signal(barrier, inc=1, device_id=(lax.rem(me + k, count), core), device_id_type=MESH)
        return _

    lax.fori_loop(1, count, greet, 0)
    for partner in near:
        pl.semaphore_signal(barrier, inc=1, device_id=partner, device_id_type=MESH)
    pl.semaphore_wait(barrier, count - 1 + len(near))

    def exchange(k, slot):
        peer = lax.rem(me + k, count)
        return pltpu.make_async_remote_copy(
            src_ref=blocks_ref.at[peer], dst_ref=recv.at[slot], send_sem=all_send.at[k],
            recv_sem=all_recv.at[k], device_id=(peer, core), device_id_type=MESH)

    def send_block(k, _):
        exchange(k, me).start()
        return _

    lax.fori_loop(1, count, send_block, 0)
    mine = pltpu.make_async_copy(blocks_ref.at[me], recv.at[me], own_sem)
    mine.start()

    factor(pairs_ref, w_ref, wt_ref, cls_ref, inc_ref, wpx_ref, lpx_ref, band, low)
    fill_filters(tile_rows, tile_cols, own_ref, left_ref, right_ref, sel_ref, tile_ref)

    def take_block(k, _):
        exchange(k, lax.rem(me + count - k, count)).wait()
        return _

    mine.wait()
    lax.fori_loop(1, count, take_block, 0)

    pixels = x_ref.shape[1]
    parts = split3(recv[...].reshape(-1, pixels) * wpx_ref[...])
    inc = inc_ref[...]
    rows[0:PAD, :] = dot_nn(inc, parts[0]) + dot_nn(inc, parts[1])
    rows[PAD:PAD + 8, :] = jnp.zeros((8, pixels), jnp.float32)

    def forward(block, carry):
        a = list(carry)
        base = pl.multiple_of(block * 8, 8)
        for s in range(8):
            at = pl.ds(base + s, 1)
            y = a[0]
            a = a[1:] + [rows[pl.ds(base + s + 8, 1), :]]
            a = [a[j] - lpx_ref[j + 1, at, :] * y for j in range(8)]
            x_ref[at, :] = y * lpx_ref[0, at, :]
        return tuple(a)

    lax.fori_loop(0, PAD // 8, forward, tuple(rows[d:d + 1, :] for d in range(8)))

    def backward(block, carry):
        later = list(carry)
        base = pl.multiple_of(block * 8, 8)
        for s in range(7, -1, -1):
            at = pl.ds(base + s, 1)
            value = x_ref[at, :]
            for g in range(8, 0, -1):
                value = value - lpx_ref[g, at, :] * later[g - 1]
            x_ref[at, :] = value
            later = [value] + later[:7]
        return tuple(later)

    def copy(i, src, dst, device):
        return pltpu.make_async_remote_copy(src_ref=src, dst_ref=dst, send_sem=send_sem.at[i],
                                            recv_sem=recv_sem.at[i], device_id=device,
                                            device_id_type=MESH)

    has_left, has_right = me > 0, me < count - 1

    @pl.when(jnp.logical_not(has_left))
    def _():
        halo_pair[0] = jnp.zeros_like(halo_pair[0])
        halo_spare[0] = jnp.zeros_like(halo_spare[0])
        halo_tile[0] = jnp.zeros_like(halo_tile[0])

    @pl.when(jnp.logical_not(has_right))
    def _():
        halo_pair[1] = jnp.zeros_like(halo_pair[1])
        halo_spare[1] = jnp.zeros_like(halo_spare[1])
        halo_tile[2] = jnp.zeros_like(halo_tile[2])

    half = pixels // 2
    total_blocks = PAD // 8
    cuts = [total_blocks * (CHUNKS - i) // CHUNKS for i in range(CHUNKS + 1)]
    carry = tuple(jnp.zeros((1, pixels), jnp.float32) for _ in range(8))
    to_left, to_right = [], []
    for i in range(CHUNKS):
        top, bottom = cuts[i], cuts[i + 1]
        carry = lax.fori_loop(0, top - bottom, lambda n, c, top=top: backward(top - 1 - n, c), carry)
        span = pl.ds(bottom * 8, (top - bottom) * 8)
        to_left.append(copy(2 * i, x_ref.at[span, pl.ds(0, half)], halo_pair.at[1, span], (left, core)))
        to_right.append(copy(2 * i + 1, x_ref.at[span, pl.ds(half, half)], halo_pair.at[0, span], (right, core)))
        if i < CHUNKS - 1:
            pl.when(has_left)(to_left[-1].start)
            pl.when(has_right)(to_right[-1].start)
    x = x_ref[...]
    edge[...] = dot_nt(sel_ref[...], x, precision=HIGHEST)
    small = [copy(2 * CHUNKS + 2 + i, edge, halo_tile.at[slot], near[i]) for i, slot in enumerate((1, 2, 0))]
    small[0].start()
    pl.when(has_left)(small[1].start)
    pl.when(has_right)(small[2].start)
    pl.when(has_left)(to_left[-1].start)
    pl.when(has_right)(to_right[-1].start)
    mid = PAD // 2
    low_lanes = iota((mid, half), 1) < half // 2
    first, second = x[:, 0:half], x[:, half:]
    spare[0] = jnp.where(low_lanes, pltpu.roll(first[0:mid], half // 2, 1), first[mid:])
    spare[1] = jnp.where(low_lanes, second[0:mid], pltpu.roll(second[mid:], half // 2, 1))
    to_right.append(copy(2 * CHUNKS, spare.at[0], halo_spare.at[0], (right, core)))
    to_left.append(copy(2 * CHUNKS + 1, spare.at[1], halo_spare.at[1], (left, core)))
    pl.when(has_right)(to_right[-1].start)
    pl.when(has_left)(to_left[-1].start)
    total = dot_nt(own_ref[...], x, precision=HIGHEST)
    small[0].wait()
    pl.when(has_left)(small[1].wait_send)
    pl.when(has_right)(small[1].wait_recv)
    pl.when(has_right)(small[2].wait_send)
    pl.when(has_left)(small[2].wait_recv)
    total += dot_nn(tile_ref[...], halo_tile[...].reshape(48, PAD), precision=HIGHEST)
    for c in to_right:
        pl.when(has_right)(c.wait_send)
        pl.when(has_left)(c.wait_recv)
    for c in to_left:
        pl.when(has_left)(c.wait_send)
        pl.when(has_right)(c.wait_recv)
    keep = (iota((PAD, half), 0) < mid) == (iota((PAD, half), 1) < half // 2)
    for side, ref in ((0, left_ref), (1, right_ref)):
        again = halo_spare[side]
        extra = jnp.where(keep, jnp.concatenate([again, again], axis=0), 0.0)
        high, middle, _ = split3(jnp.concatenate([halo_pair[side], extra], axis=1))
        total = total + (dot_nt(ref[0], high) + (dot_nt(ref[0], middle) + dot_nt(ref[1], high)))
    out_ref[...] = total[:, 0:DATES]


def on_device(phases, pairs, class_weights, classes):
    own_ifg, tile_rows, cols = phases.shape
    tile_cols = classes.shape[1]
    pixels = tile_rows * tile_cols
    count = cols // tile_cols
    nifg = pairs.shape[0]
    half = pixels // 2
    vmem = pl.BlockSpec(memory_space=pltpu.VMEM)
    f32, bf16 = jnp.float32, jnp.bfloat16
    copies = 2 * CHUNKS + 5

    blocks = phases.transpose(0, 2, 1).reshape(own_ifg, count, pixels).transpose(1, 0, 2)
    padded = jnp.pad(class_weights, ((0, LANES - CLASSES), (0, 0)))
    corrected = pl.pallas_call(
        functools.partial(kernel, tile_rows, tile_cols),
        out_shape=jax.ShapeDtypeStruct((pixels, DATES), f32),
        in_specs=[vmem] * 5,
        out_specs=vmem,
        scratch_shapes=[
            pltpu.VMEM((count, own_ifg, pixels), f32),
            pltpu.VMEM((PAD, nifg), bf16),
            pltpu.VMEM((nifg, pixels), f32),
            pltpu.VMEM((MAXGAP + 1, PAD, pixels), f32),
            pltpu.VMEM((MAXGAP + 1, PAD, LANES), f32),
            pltpu.VMEM((MAXGAP + 1, PAD, LANES), f32),
            pltpu.VMEM((pixels, pixels), f32),
            pltpu.VMEM((2, pixels, pixels), bf16),
            pltpu.VMEM((2, pixels, pixels), bf16),
            pltpu.VMEM((16, pixels), f32),
            pltpu.VMEM((pixels, 48), f32),
            pltpu.VMEM((PAD + 8, pixels), f32),
            pltpu.VMEM((PAD, pixels), f32),
            pltpu.VMEM((2, PAD // 2, half), f32),
            pltpu.VMEM((16, PAD), f32),
            pltpu.VMEM((2, PAD, half), f32),
            pltpu.VMEM((2, PAD // 2, half), f32),
            pltpu.VMEM((3, 16, PAD), f32),
            pltpu.SemaphoreType.DMA((count,)),
            pltpu.SemaphoreType.DMA((count,)),
            pltpu.SemaphoreType.DMA,
            pltpu.SemaphoreType.DMA((copies,)),
            pltpu.SemaphoreType.DMA((copies,)),
        ],
        compiler_params=pltpu.CompilerParams(
            collective_id=0, has_side_effects=True, vmem_limit_bytes=48 * 1024 * 1024
        ),
        name="invert_and_filter",
    )(blocks, pairs.T, padded, padded.T, classes.T.reshape(1, pixels))
    return corrected.reshape(tile_rows, tile_cols, DATES)


def solution(mesh):
    return jax.shard_map(
        on_device,
        mesh=mesh,
        in_specs=(P("ifg", "tile", None), P(), P(), P("tile", "ifg")),
        out_specs=P("tile", "ifg", None),
        check_vma=False,
    )
```
